512 devices in a mesh: tenant: 32 (over z, x), tensor: 16 (over y, core).
Axes of the slice: x: 4, y: 8, z: 8, core: 2. Of those that a mesh axis runs over, the one named last changes fastest.
Arguments:
- activations: bfloat16 [1536, 8192], P('tenant', 'tensor'), may hold values from -6 to 6
- base_weight: bfloat16 [8192, 28672], P('tensor', 'tenant'), may hold values from -0.0625 to 0.0625
- v_codes: int32 [32, 8192, 256], P('tenant', 'tensor'), may hold values from 0 to 255, as said below
- u_codes: int32 [32, 256, 28672], P('tenant', 'tensor'), may hold values from 0 to 255, as said below
- group_bits: int32 [32, 8], P('tenant'), may hold values from 2 to 8, as said below
- v_scale: float32 [32, 256], P('tenant'), may hold values from 0.0055242716 to 0.044194173
- u_scale: float32 [32, 256], P('tenant', 'tensor'), may hold values from 0.015625 to 0.125
- tenant_of: int32 [1536, 1], replicated, may hold values from 0 to 19; in each aligned block of 1536 rows (0 to 1535, 1536 to 3071, ...) at most 96 rows name the same one
- owner_map: int32 [20], replicated, may hold values from 0 to 31, as said below
Outputs:
- projected: bfloat16 [1536, 28672], P('tensor', 'tenant')
The draws below stay inside these ranges and needn't reach their ends.
Inputs may be any that keep to these rules, and one draw needn't show every extreme that they name: `tenant_of`: no tenant has more than 96 rows, some tenant has exactly 96, and every tenant has at least one row. `owner_map`: distinct owners for distinct tenants. `group_bits`: for each owner the first group has 8 bits, the next one to four groups 3 bits, the rest 2 bits. `v_codes`: A code of rank index r lies in 0 to 2 ** group_bits[o, r // 32] - 1. `u_codes`: A code of rank index r lies in 0 to 2 ** group_bits[o, r // 32] - 1.
All inputs are finite; a program needn't handle non-finite values.
Results may differ from the reference program's by a relative error of at most 0.03.
Values may be sent and summed in bfloat16 or wider, within the bound.
A program may use at most 128 MiB of HBM per device.

```python
import math
import jax
import jax.numpy as jnp
import numpy as np
from jax import lax

D = 8192
FF = 28672
R = 256
GROUPS = 8
CAP = 96
ROWS = 1536
TENANTS = 20
N_TENANT = 32
N_TENSOR = 16


def level_bits(key):
    key = jax.random.fold_in(key, 101)
    threes = jax.random.randint(key, (N_TENANT, 1), 1, 5)
    group_order = jnp.arange(GROUPS)[None, :]
    return jnp.where(group_order == 0, 8, jnp.where(group_order <= threes, 3, 2)).astype(jnp.int32)


def draw_group_bits(key, part):
    return level_bits(key)


def draw_v_codes(key, part):
    levels = jnp.left_shift(jnp.ones((N_TENANT, GROUPS), jnp.int32), level_bits(key))
    key = jax.random.fold_in(key, 3)
    rank_levels = jnp.repeat(levels, R // GROUPS, axis=1)
    raw_bits = jax.random.randint(key, (N_TENANT, D, R), 0, 2 ** 30)
    return (raw_bits % rank_levels[:, None, :]).astype(jnp.int32)


def draw_u_codes(key, part):
    levels = jnp.left_shift(jnp.ones((N_TENANT, GROUPS), jnp.int32), level_bits(key))
    key = jax.random.fold_in(key, 5)
    rank_levels = jnp.repeat(levels, R // GROUPS, axis=1)
    raw_bits = jax.random.randint(key, (N_TENANT, R, FF), 0, 2 ** 30)
    return (raw_bits % rank_levels[:, :, None]).astype(jnp.int32)


def draw_owner_map(key, part):
    key = jax.random.fold_in(key, 7)
    first_key, second_key = jax.random.split(key)
    middle = jax.random.permutation(first_key, N_TENANT - 2)[:TENANTS - 2] + 1
    chosen = jnp.concatenate([jnp.array([0, N_TENANT - 1], jnp.int32), middle.astype(jnp.int32)])
    return jax.random.permutation(second_key, chosen).astype(jnp.int32)


def steps_of(own_key, shape, shards, smallest, high):
    level, own = 1.0, jax.random.fold_in(own_key, 6)
    for position, shards_of in shards:
        draws = jnp.exp(jax.random.uniform(jax.random.fold_in(own, position), (shards_of,), jnp.float32, smallest / len(shards), high / len(shards)))
        level = level * jnp.repeat(draws, shape[position] // shards_of).reshape([-1 if axis == position else 1 for axis in range(len(shape))])
    return level


def routed_block(stream_key, own, number, rows, count, top, bound, lean):
    sequence = jax.random.permutation(stream_key, count)
    crowded, common = portions_of(count, rows * top, bound, lean, True), portions_of(count, rows * top, bound, lean, False)
    places = jnp.arange(count)

    def named(sizes, rotation):
        used = int((sizes > 0).sum())
        fixed = max(1, used // 4)
        moved = fixed + (places - fixed + rotation * (used - fixed)) % max(1, count - fixed)
        return jnp.zeros((count,), jnp.int32).at[sequence[jnp.where(places < fixed, places, moved)]].set(jnp.asarray(sizes, jnp.int32))

    sizes = jnp.where(number % 4 == 0, named(crowded, number // 4), named(common, number - number // 4 - 1))
    mixed = jax.random.permutation(jax.random.fold_in(own, 3), count)
    source_of, sink = mixed[0:count // 2 * 2:2], mixed[1:count // 2 * 2:2]
    room = jnp.minimum(sizes[source_of] - 1, bound - sizes[sink]) // 2
    room = jnp.where((source_of == sequence[0]) | (sink == sequence[0]) | (sizes[sink] == 0), 0, jnp.maximum(room, 0))
    moved = jax.random.randint(jax.random.fold_in(own, 4), (count // 2,), 0, 1 << 20) % (room + 1)
    sizes = sizes.at[source_of].add(-moved).at[sink].add(moved)
    members = jnp.searchsorted(jnp.cumsum(sizes), jnp.arange(rows * top), side="right").astype(jnp.int32)
    table = members.reshape(top, rows).T
    table = table[jax.random.permutation(jax.random.fold_in(own, 1), rows)]
    rotation = jax.random.randint(jax.random.fold_in(own, 2), (rows, 1), 0, top)
    return jnp.take_along_axis(table, (jnp.arange(top)[None, :] + rotation) % top, axis=1)


def portions_of(count, total, reach, skew, full):
    portions = [(1 << 20) // math.isqrt(grade ** skew) + 1 for grade in range(1, count + 1)]
    largest = reach if full else min(reach, max(-(-total // count), total * portions[0] // sum(portions)))
    least = 1 if total - largest >= count - 1 else 0
    given, rest = [largest] + [least] * (count - 1), total - largest - least * (count - 1)
    while rest > 0:
        free = [i for i in range(1, count) if given[i] < largest] or [i for i in range(1, count) if given[i] < reach]
        whole, left = sum([portions[i] for i in free]), rest
        for i in free:
            addition = min(reach - given[i], max(1, left * portions[i] // whole), rest)
            given[i] = given[i] + addition
            rest = rest - addition
    return np.array(given)


def gaussian(stream_key, shape, deviation, limit, shards=(), kind=jnp.bfloat16):
    values = jax.random.normal(stream_key, shape, jnp.float32) * deviation
    if len(shards) > 0:
        values = steps_of(stream_key, shape, shards, -0.22, 0.18) * values
    return jnp.clip(values, min=-limit, max=limit).astype(kind)


def setup_inputs(seed: int = 0) -> dict:
    streams_of = jax.random.split(jax.random.key(seed), 10)
    activations = gaussian(streams_of[0], (ROWS, D), 1.0, 6.0, ((0, 32), (1, 16)))
    base_weight = gaussian(streams_of[1], (D, FF), D ** -0.5, 0.0625, ((0, 16), (1, 32)))
    v_codes = draw_v_codes(jax.random.fold_in(streams_of[9], 71), 0)
    u_codes = draw_u_codes(jax.random.fold_in(streams_of[9], 71), 0)
    group_bits = draw_group_bits(jax.random.fold_in(streams_of[9], 71), 0)
    v_scale = jnp.clip(jnp.exp(math.log(0.044194173) - 2.0794415 * jax.random.uniform(streams_of[5], (N_TENANT, R), jnp.float32) ** steps_of(streams_of[5], (N_TENANT, R), ((0, 32),), -0.2, 0.2)), 0.0055242716, 0.044194173)
    u_scale = jnp.clip(jnp.exp(math.log(0.125) - 2.0794415 * jax.random.uniform(streams_of[6], (N_TENANT, R), jnp.float32) ** steps_of(streams_of[6], (N_TENANT, R), ((0, 32), (1, 16)), -0.2, 0.2)), 0.015625, 0.125)
    tenant_of_keys = jax.random.split(jax.random.fold_in(streams_of[7], 1), ROWS // ROWS)
    tenant_of_turns = jax.random.permutation(jax.random.fold_in(streams_of[7], 3), ROWS // ROWS)
    tenant_of = jax.vmap(lambda own, number: routed_block(jax.random.fold_in(streams_of[7], 2), own, number, ROWS, TENANTS, 1, CAP, 2))(tenant_of_keys, tenant_of_turns).reshape((ROWS, 1))
    owner_map = draw_owner_map(jax.random.fold_in(streams_of[9], 71), 0)
    return {"activations": activations, "base_weight": base_weight, "v_codes": v_codes, "u_codes": u_codes, "group_bits": group_bits, "v_scale": v_scale, "u_scale": u_scale, "tenant_of": tenant_of, "owner_map": owner_map}


def column_levels(bits_row, span_size, first_row, group_size):
    positions = first_row + jnp.arange(span_size, dtype=jnp.int32)
    group_ids = positions // group_size
    level_table = jnp.left_shift(jnp.ones_like(bits_row), bits_row)
    in_group = group_ids[:, None] == jnp.arange(bits_row.shape[0], dtype=jnp.int32)[None, :]
    return jnp.sum(jnp.where(in_group, level_table[None, :], 0), axis=1).astype(jnp.int32)


def dequantize(code_block, level_col, col_scale):
    spread = (level_col - 1).astype(jnp.float32)
    centered = 2.0 * code_block.astype(jnp.float32) - spread
    return (centered / spread * col_scale).astype(jnp.bfloat16)


def reference(activations, base_weight, v_codes, u_codes, group_bits, v_scale, u_scale, tenant_of, owner_map):
    tenant_ids = tenant_of[:, 0]
    member = (tenant_ids[:, None] == jnp.arange(TENANTS, dtype=jnp.int32)[None, :]).astype(jnp.int32)
    slot_index = (jnp.sum(jnp.cumsum(member, axis=0) * member, axis=1) - 1).astype(jnp.int32)
    row_ids = jnp.arange(ROWS, dtype=jnp.int32)
    group_size = R // GROUPS
    d_local = D // N_TENSOR
    rank_local = R // N_TENSOR
    rank_codes = []
    u_list = []
    slot_lists = []
    for tenant in range(TENANTS):
        owner = owner_map[tenant]
        targets = jnp.where(tenant_ids == tenant, slot_index, CAP).astype(jnp.int32)
        chosen_rows = jnp.full((CAP,), ROWS, jnp.int32).at[targets].set(row_ids, mode="drop")
        picked = jnp.take(activations, chosen_rows, axis=0, mode="clip")
        levels = column_levels(group_bits[owner], R, 0, group_size)
        v_deq = dequantize(v_codes[owner], levels[None, :], v_scale[owner][None, :])
        rank_codes.append(jnp.dot(picked, v_deq, preferred_element_type=jnp.float32).astype(jnp.bfloat16))
        u_list.append(dequantize(u_codes[owner], levels[:, None], u_scale[owner][:, None]))
        slot_lists.append(chosen_rows)
    projected = jnp.zeros((ROWS, FF), jnp.float32)
    for slice_index in range(N_TENSOR):
        d_low = slice_index * d_local
        r_low = slice_index * rank_local
        running = jnp.dot(activations[:, d_low:d_low + d_local], base_weight[d_low:d_low + d_local], preferred_element_type=jnp.float32)
        for tenant in range(TENANTS):
            delta = jnp.dot(rank_codes[tenant][:, r_low:r_low + rank_local], u_list[tenant][r_low:r_low + rank_local], preferred_element_type=jnp.float32)
            running = running.at[slot_lists[tenant]].add(delta, mode="drop")
        projected = projected + lax.optimization_barrier(running.astype(jnp.bfloat16)).astype(jnp.float32)
    return projected.astype(jnp.bfloat16)
```

```python
import functools

import jax
import jax.numpy as jnp
from jax import lax
from jax.experimental import pallas as pl
from jax.experimental.pallas import tpu as pltpu
from jax.sharding import PartitionSpec as P

MESH = pl.DeviceIdType.MESH
BF16, F32, I32 = jnp.bfloat16, jnp.float32, jnp.int32

NX, NC = 4, 2
SLOTS = 128
Z_ORDER = (0, -1, 1, -2, 2, -3, 3, -4)


def kernel(
    act, w_hbm, vc_hbm, uc_hbm, bits, v_scale, u_scale, tenant, owner_map, out,
    g, w, vc, uc, uq, vq, ur, rank_out, rank_in, code, codes, slot_hot, row_owner, slot_key,
    acc, sib_out, sib_in, ring_up, ring_dn,
    load_sem, a_send, a_recv, u_send, u_recv, r_send, r_recv, c_send, c_recv,
    x_send, x_recv, up_send, up_recv, dn_send, dn_recv,
    *, n_tenant, n_tensor,
):
    t, s = lax.axis_index("tenant"), lax.axis_index("tensor")
    nz, ny = n_tenant // NX, n_tensor // NC
    z, x = t // NX, t % NX
    y, c = s // NC, s % NC
    rows_t, depth = act.shape
    rows = g.shape[0]
    cols = w.shape[1]
    rank_local = uc.shape[0]
    full_rank = vc.shape[1]
    n_tenants = owner_map.shape[0]
    group = full_rank // bits.shape[1]
    rows_s = out.shape[0]

    def remote(src, dst, send_sem, recv_sem, device):
        return pltpu.make_async_remote_copy(
            src_ref=src, dst_ref=dst, send_sem=send_sem, recv_sem=recv_sem,
            device_id=device, device_id_type=MESH,
        )

    def wait_bytes(ref, sem):
        pltpu.make_async_copy(ref, ref, sem).wait()

    loads = [
        pltpu.make_async_copy(uc_hbm.at[0], uc, load_sem.at[0]),
        pltpu.make_async_copy(vc_hbm.at[0], vc, load_sem.at[1]),
        pltpu.make_async_copy(w_hbm, w, load_sem.at[2]),
        pltpu.make_async_copy(act, g.at[pl.ds(t * rows_t, rows_t)], load_sem.at[3]),
    ]
    for load in loads:
        load.start()

    barrier = pltpu.get_barrier_semaphore()

    def greet_tenant(i, carry):
        pl.semaphore_signal(barrier, 1, device_id=((t + i) % n_tenant, s), device_id_type=MESH)
        return carry

    def greet_tensor(i, carry):
        pl.semaphore_signal(barrier, 1, device_id=(t, (s + i) % n_tensor), device_id_type=MESH)
        return carry

    lax.fori_loop(1, n_tenant, greet_tenant, 0)
    lax.fori_loop(1, n_tensor, greet_tensor, 0)

    u_spread = (jnp.left_shift(1, bits[0, s * rank_local // group]) - 1).astype(F32)
    diagonal = lax.broadcasted_iota(I32, (rank_local, rank_local), 0) == lax.broadcasted_iota(
        I32, (rank_local, rank_local), 1
    )
    u_factor = (
        jnp.sum(jnp.where(diagonal, u_scale[...], 0.0), axis=1, keepdims=True) / u_spread
    )
    loads[0].wait()

    def dequantize_u(i, carry):
        block = uc[:, pl.ds(pl.multiple_of(i * cols, 128), cols)]
        uq[i] = ((2.0 * block.astype(F32) - u_spread) * u_factor).astype(BF16)
        return carry

    lax.fori_loop(0, n_tenant, dequantize_u, 0)

    pl.semaphore_wait(barrier, n_tenant + n_tensor - 2)

    def block_at(dz, dx):
        return ((z + dz + nz) % nz) * NX + (x + dx + NX) % NX

    up, dn, right, left = block_at(1, 0), block_at(-1, 0), block_at(0, 1), block_at(0, -1)

    def g_at(block):
        return g.at[pl.ds(block * rows_t, rows_t)]

    def send_block(block, to, src=None):
        remote(
            g_at(block) if src is None else src, g_at(block), a_send, a_recv.at[block], (to, s)
        ).start()

    def wait_block(block):
        wait_bytes(g_at(block), a_recv.at[block])

    def send_u(i, carry):
        to = (t + i) % n_tenant
        remote(uq.at[to], ur.at[pl.ds(t * rank_local, rank_local)], u_send, u_recv, (to, s)).start()
        return carry

    for to in (up, dn, right, left):
        send_block(t, to, act)

    def relay(j):
        if j % 2 == 0:
            block = block_at(Z_ORDER[j], -1)
            wait_block(block)
            send_block(block, right)
        else:
            block = block_at(Z_ORDER[j], 1)
            wait_block(block)
            send_block(block, left)

    lax.fori_loop(1, 4, send_u, 0)
    lane = lax.broadcasted_iota(I32, (1, full_rank), 1)
    v_spread = jnp.zeros((1, full_rank), F32)
    for i in range(bits.shape[1]):
        spread = (jnp.left_shift(1, bits[0, i]) - 1).astype(F32)
        v_spread = jnp.where(lane // group == i, spread, v_spread)
    v_factor = v_scale[...] / v_spread
    loads[1].wait()
    vq[...] = ((2.0 * vc[...].astype(F32) - v_spread) * v_factor).astype(BF16)

    for j in range(1, nz):
        dz = Z_ORDER[j]
        block = block_at(dz, 0)
        wait_block(block)
        if -4 < dz < 0:
            send_block(block, up)
        if 0 < dz < 3:
            send_block(block, dn)
        send_block(block, right)
        send_block(block, left)
        relay(j - 1)
        lax.fori_loop(4 * j, 4 * j + 4, send_u, 0)
    relay(nz - 1)

    tri = (
        lax.broadcasted_iota(I32, (128, 128), 0) <= lax.broadcasted_iota(I32, (128, 128), 1)
    ).astype(BF16)
    carry = jnp.zeros((32, 1), F32)
    for b in range(rows // 128):
        ids = tenant[:, b * 128:(b + 1) * 128]
        member = (lax.broadcasted_iota(I32, (32, 128), 0) == ids).astype(F32)
        count = carry + jnp.dot(member.astype(BF16), tri, preferred_element_type=F32)
        carry = count[:, 127:128]
        slot = jnp.sum(count * member, axis=0, keepdims=True) - 1.0
        owner = jnp.zeros((1, 128), F32)
        for i in range(n_tenants):
            owner = jnp.where(ids == i, owner_map[i].astype(F32), owner)
        key = owner * float(SLOTS) + slot
        slot_key[:, b * 128:(b + 1) * 128] = key.astype(I32)
        column = jnp.transpose(jnp.broadcast_to(key, (128, 128))).astype(I32)
        slot_hot[b * 128:(b + 1) * 128, :] = (
            column % SLOTS == lax.broadcasted_iota(I32, (128, 128), 1)
        ).astype(BF16)
        row_owner[b * 128:(b + 1) * 128, :] = column // SLOTS

    loads[3].wait()
    for j in range(nz):
        wait_block(block_at(Z_ORDER[j], 1 if j % 2 == 0 else -1))
        wait_block(block_at(Z_ORDER[j], 2))

    pick = (
        slot_key[...] == t * SLOTS + lax.broadcasted_iota(I32, (SLOTS, rows), 0)
    ).astype(BF16)
    picked = jnp.dot(pick, g[...], preferred_element_type=F32).astype(BF16)
    part = jnp.dot(picked, vq[...], preferred_element_type=F32)
    rank_out[...] = jnp.transpose(part).astype(BF16)

    def send_rank(i, carry):
        to = (s + i) % n_tensor
        remote(
            rank_out.at[pl.ds(to * rank_local, rank_local)],
            rank_in.at[pl.ds(s * rank_local, rank_local)],
            r_send, r_recv, (t, to),
        ).start()
        return carry

    lax.fori_loop(1, n_tensor, send_rank, 0)
    mine = pl.ds(pl.multiple_of(s * rank_local, rank_local), rank_local)
    rank_in[mine, :] = rank_out[mine, :]

    loads[2].wait()
    step = 2 * rows_s
    half = rows // step // 2

    def shared(i, carry):
        here = pl.ds(pl.multiple_of(i * step, step), step)
        acc[here, :] = jnp.dot(g[here, :], w[...], preferred_element_type=F32)
        return carry

    lax.fori_loop(0, half, shared, 0)

    wait_bytes(rank_in.at[pl.ds(0, (n_tensor - 1) * rank_local)], r_recv)
    total = jnp.zeros((rank_local, SLOTS), F32)
    for i in range(n_tensor):
        total = total + rank_in[i * rank_local:(i + 1) * rank_local, :].astype(F32)
    code[...] = total.astype(BF16)

    def send_code(i, carry):
        to = (t + i) % n_tenant
        remote(code, codes.at[pl.ds(t * rank_local, rank_local)], c_send, c_recv, (to, s)).start()
        return carry

    lax.fori_loop(1, n_tenant, send_code, 0)
    here_t = pl.ds(pl.multiple_of(t * rank_local, rank_local), rank_local)
    codes[here_t, :] = code[...]
    ur[here_t, :] = uq[t]

    lax.fori_loop(half, 2 * half, shared, 0)

    others = pl.ds(0, (n_tenant - 1) * rank_local)
    wait_bytes(codes.at[others], c_recv)
    wait_bytes(ur.at[others], u_recv)

    owner_lane = lax.broadcasted_iota(I32, (step, n_tenant * rank_local), 1) // rank_local

    def ring_block(j):
        away = (j // 2 + 1) * (1 - j // (ny - 1))
        return (y + (2 * (j % 2) - 1) * away + ny) % ny

    def terms(j, carry):
        d = ring_block(j)
        here = pl.ds(pl.multiple_of(d * step, step), step)
        spread_codes = lax.dot_general(
            slot_hot[here, :], codes[...], (((1,), (1,)), ((), ())), preferred_element_type=F32
        )
        owner = row_owner[here, :]
        owner = jnp.concatenate([owner] * (n_tenant * rank_local // 128), axis=1)
        spread_codes = jnp.where(owner == owner_lane, spread_codes, 0.0).astype(BF16)
        value = acc[here, :] + jnp.dot(spread_codes, ur[...], preferred_element_type=F32)
        acc[here, :] = value
        theirs = pl.ds(pl.multiple_of(d * step + (1 - c) * rows_s, rows_s), rows_s)
        sib_out[d] = acc[theirs, :].astype(BF16)
        remote(sib_out.at[d], sib_in.at[d], x_send, x_recv.at[d], (t, y * NC + 1 - c)).start()
        return carry

    lax.fori_loop(0, ny, terms, 0)

    piece = 16
    pieces = rows_s // 2 // piece
    y_up, y_dn = ((y + 1) % ny) * NC + c, ((y + ny - 1) % ny) * NC + c

    def chip_sum(d, first):
        here = pl.ds(pl.multiple_of(d * step + c * rows_s + first, piece), piece)
        return acc[here, :] + sib_in[d, first:first + piece, :].astype(F32)

    def ring_step(k, carry):
        for p in range(pieces):
            for way in range(2):
                d = (y + ny - 1 - k) % ny if way == 0 else (y + 1 + k) % ny
                first = (way * pieces + p) * piece
                slots, send, recv, to = (
                    (ring_up, up_send, up_recv, (t, y_up))
                    if way == 0
                    else (ring_dn, dn_send, dn_recv, (t, y_dn))
                )
                lines = pl.ds(p * piece, piece)
                wait_bytes(slots.at[k - 1, lines], recv.at[k - 1, p])
                slots[k - 1, lines, :] = (
                    slots[k - 1, lines, :].astype(F32) + chip_sum(d, first)
                ).astype(BF16)
                remote(
                    slots.at[k - 1, lines], slots.at[k, lines], send, recv.at[k, p], to
                ).start()
        return carry

    start_up, start_dn = (y + ny - 1) % ny, (y + 1) % ny
    wait_bytes(sib_in.at[start_up], x_recv.at[start_up])
    wait_bytes(sib_in.at[start_dn], x_recv.at[start_dn])
    for p in range(pieces):
        lines = pl.ds(p * piece, piece)
        ring_up[ny - 1, lines, :] = chip_sum(start_up, p * piece).astype(BF16)
        remote(
            ring_up.at[ny - 1, lines], ring_up.at[0, lines], up_send, up_recv.at[0, p], (t, y_up)
        ).start()
        ring_dn[ny - 1, lines, :] = chip_sum(start_dn, (pieces + p) * piece).astype(BF16)
        remote(
            ring_dn.at[ny - 1, lines], ring_dn.at[0, lines], dn_send, dn_recv.at[0, p], (t, y_dn)
        ).start()

    def wait_sibling(j, carry):
        d = ring_block(j)
        wait_bytes(sib_in.at[d], x_recv.at[d])
        return carry

    lax.fori_loop(2, ny, wait_sibling, 0)
    lax.fori_loop(1, ny - 1, ring_step, 0)
    for p in range(pieces):
        for way in range(2):
            slots, recv = (ring_up, up_recv) if way == 0 else (ring_dn, dn_recv)
            first = (way * pieces + p) * piece
            lines = pl.ds(p * piece, piece)
            wait_bytes(slots.at[ny - 2, lines], recv.at[ny - 2, p])
            out[first:first + piece, :] = (
                slots[ny - 2, lines, :].astype(F32) + chip_sum(y, first)
            ).astype(BF16)

    wait_bytes(g.at[pl.ds(0, (n_tenant - 1) * rows_t)], a_send)
    wait_bytes(ur.at[others], u_send)
    wait_bytes(rank_in.at[pl.ds(0, (n_tensor - 1) * rank_local)], r_send)
    wait_bytes(codes.at[others], c_send)
    wait_bytes(sib_out, x_send)
    wait_bytes(ring_up.at[pl.ds(0, ny - 1)], up_send)
    wait_bytes(ring_dn.at[pl.ds(0, ny - 1)], dn_send)


def on_device(
    n_tenant, n_tensor,
    activations, base_weight, v_codes, u_codes, group_bits, v_scale, u_scale, tenant_of, owner_map,
):
    rows_t, depth = activations.shape
    cols = base_weight.shape[1]
    rows = tenant_of.shape[0]
    full_rank = v_codes.shape[2]
    rank_local = u_codes.shape[1]
    rows_s = rows // n_tensor
    ny = n_tensor // NC
    all_ranks = n_tenant * rank_local
    vmem = pl.BlockSpec(memory_space=pltpu.VMEM)
    smem = pl.BlockSpec(memory_space=pltpu.SMEM)
    hbm = pl.BlockSpec(memory_space=pl.ANY)
    dma = pltpu.SemaphoreType.DMA
    pieces = rows_s // 2 // 16
    return pl.pallas_call(
        functools.partial(kernel, n_tenant=n_tenant, n_tensor=n_tensor),
        out_shape=jax.ShapeDtypeStruct((rows_s, cols), BF16),
        in_specs=[hbm, hbm, hbm, hbm, smem, vmem, vmem, vmem, smem],
        out_specs=vmem,
        scratch_shapes=[
            pltpu.VMEM((rows, depth), BF16),
            pltpu.VMEM((depth, cols), BF16),
            pltpu.VMEM((depth, full_rank), I32),
            pltpu.VMEM(u_codes.shape[1:], I32),
            pltpu.VMEM((n_tenant, rank_local, cols), BF16),
            pltpu.VMEM((depth, full_rank), BF16),
            pltpu.VMEM((all_ranks, cols), BF16),
            pltpu.VMEM((full_rank, SLOTS), BF16),
            pltpu.VMEM((full_rank, SLOTS), BF16),
            pltpu.VMEM((rank_local, SLOTS), BF16),
            pltpu.VMEM((all_ranks, SLOTS), BF16),
            pltpu.VMEM((rows, SLOTS), BF16),
            pltpu.VMEM((rows, 128), I32),
            pltpu.VMEM((1, rows), I32),
            pltpu.VMEM((rows, cols), F32),
            pltpu.VMEM((ny, rows_s, cols), BF16),
            pltpu.VMEM((ny, rows_s, cols), BF16),
            pltpu.VMEM((ny, rows_s // 2, cols), BF16),
            pltpu.VMEM((ny, rows_s // 2, cols), BF16),
            dma((4,)), dma, dma((n_tenant,)), dma, dma, dma, dma, dma, dma,
            dma, dma((ny,)), dma, dma((ny - 1, pieces)), dma, dma((ny - 1, pieces)),
        ],
        compiler_params=pltpu.CompilerParams(
            collective_id=0, has_side_effects=True, vmem_limit_bytes=48 * 1024 * 1024
        ),
        name="up_projection",
    )(
        activations, base_weight, v_codes, u_codes, group_bits, v_scale, u_scale,
        tenant_of.reshape(1, rows), owner_map,
    )


def solution(mesh):
    in_specs = (
        P("tenant", "tensor"),
        P("tensor", "tenant"),
        P("tenant", "tensor", None),
        P("tenant", "tensor", None),
        P("tenant", None),
        P("tenant", None),
        P("tenant", "tensor"),
        P(),
        P(),
    )
    return jax.shard_map(
        functools.partial(on_device, mesh.shape["tenant"], mesh.shape["tensor"]),
        mesh=mesh, in_specs=in_specs, out_specs=P("tensor", "tenant"), check_vma=False,
    )
```

```python
import functools

import jax
import jax.numpy as jnp
from jax import lax
from jax.experimental import pallas as pl
from jax.experimental.pallas import tpu as pltpu
from jax.sharding import PartitionSpec as P

MESH = pl.DeviceIdType.MESH
BF16, F32, I32 = jnp.bfloat16, jnp.float32, jnp.int32

NX, NC = 4, 2
SLOTS = 128
Z_ORDER = (0, -1, 1, -2, 2, -3, 3, -4)
RELAYED = 6
LAG = 3
PIECE = 16
Y_FAR_FIRST = (4, 3, -3, 2, -2, 1, -1)
T_FAR_FIRST = tuple(
    sorted(
        ((dz, dx) for dz in Z_ORDER for dx in (0, 1, -1, 2) if (dz, dx) != (0, 0)),
        key=lambda at: -abs(at[0]) - abs(at[1]),
    )
)


def kernel(
    act, w_hbm, vc_hbm, uc_hbm, bits, v_scale, u_scale, tenant, owner_map, out,
    g, w, vc, uc, uq, vq, ur, rank_out, rank_sib, rank_sum, rank_in, code, codes,
    slot_hot, row_owner, slot_key, acc, sib_out, sib_in, stage, ring_up, ring_dn,
    load_sem, a_send, a_recv, u_send, u_recv, q_send, q_recv, r_send, r_recv, c_send, c_recv,
    x_send, x_recv, up_send, up_recv, dn_send, dn_recv, token,
    *, n_tenant, n_tensor,
):
    t, s = lax.axis_index("tenant"), lax.axis_index("tensor")
    nz, ny = n_tenant // NX, n_tensor // NC
    z, x = t // NX, t % NX
    y, c = s // NC, s % NC
    rows_t, depth = act.shape
    rows = g.shape[0]
    cols = w.shape[1]
    rank_local = uc.shape[0]
    full_rank = vc.shape[1]
    n_tenants = owner_map.shape[0]
    group = full_rank // bits.shape[1]
    rows_s = out.shape[0]

    def remote(src, dst, send_sem, recv_sem, device):
        return pltpu.make_async_remote_copy(
            src_ref=src, dst_ref=dst, send_sem=send_sem, recv_sem=recv_sem,
            device_id=device, device_id_type=MESH,
        )

    def wait_bytes(ref, sem):
        pltpu.make_async_copy(ref, ref, sem).wait()

    def at_tenant(dz, dx):
        return ((z + dz + nz) % nz) * NX + (x + dx + NX) % NX

    def at_tensor(dy):
        return ((y + dy + ny) % ny) * NC + c

    up, dn, right, left = at_tenant(1, 0), at_tenant(-1, 0), at_tenant(0, 1), at_tenant(0, -1)
    y_up, y_dn, sibling = at_tensor(1), at_tensor(-1), y * NC + 1 - c

    loads = [
        pltpu.make_async_copy(uc_hbm.at[0], uc, load_sem.at[0]),
        pltpu.make_async_copy(vc_hbm.at[0], vc, load_sem.at[1]),
        pltpu.make_async_copy(w_hbm, w, load_sem.at[2]),
        pltpu.make_async_copy(act, g.at[pl.ds(t * rows_t, rows_t)], load_sem.at[3]),
    ]
    for load in loads:
        load.start()

    barrier = pltpu.get_barrier_semaphore()
    for device in (
        (up, s), (dn, s), (right, s), (left, s), (t, y_up), (t, y_dn), (t, sibling),
    ):
        pl.semaphore_signal(barrier, 1, device_id=device, device_id_type=MESH)

    u_spread = (jnp.left_shift(1, bits[0, s * rank_local // group]) - 1).astype(F32)
    diagonal = lax.broadcasted_iota(I32, (rank_local, rank_local), 0) == lax.broadcasted_iota(
        I32, (rank_local, rank_local), 1
    )
    u_factor = (
        jnp.sum(jnp.where(diagonal, u_scale[...], 0.0), axis=1, keepdims=True) / u_spread
    )
    loads[0].wait()

    def dequantize_u(i, carry):
        block = uc[:, pl.ds(pl.multiple_of(i * cols, 128), cols)]
        uq[i] = ((2.0 * block.astype(F32) - u_spread) * u_factor).astype(BF16)
        return carry

    lax.fori_loop(0, n_tenant, dequantize_u, 0)

    lane = lax.broadcasted_iota(I32, (1, full_rank), 1)
    v_spread = jnp.zeros((1, full_rank), F32)
    for i in range(bits.shape[1]):
        spread = (jnp.left_shift(1, bits[0, i]) - 1).astype(F32)
        v_spread = jnp.where(lane // group == i, spread, v_spread)
    v_factor = v_scale[...] / v_spread
    loads[1].wait()
    vq[...] = ((2.0 * vc[...].astype(F32) - v_spread) * v_factor).astype(BF16)
    loads[2].wait()
    loads[3].wait()

    pl.semaphore_wait(barrier, 7)

    def g_at(block):
        return g.at[pl.ds(block * rows_t, rows_t)]

    def send_block(block, to):
        remote(g_at(block), g_at(block), a_send, a_recv.at[block], (to, s)).start()

    def wait_block(block):
        wait_bytes(g_at(block), a_recv.at[block])

    def send_u(to):
        remote(uq.at[to], ur.at[pl.ds(t * rank_local, rank_local)], u_send, u_recv, (to, s)).start()

    def across(block, j):
        send_block(block, right)
        send_block(block, left)
        if j >= RELAYED:
            send_block(block, at_tenant(0, 2))

    def relay(j):
        if 0 <= j < RELAYED:
            block = at_tenant(Z_ORDER[j], -1 if j % 2 == 0 else 1)
            wait_block(block)
            send_block(block, right if j % 2 == 0 else left)
            send_u(block)

    def greet(i):
        for device in ((t, y_up), (t, y_dn)):
            pl.semaphore_signal(token.at[i], 1, device_id=device, device_id_type=MESH)

    send_block(t, up)
    send_block(t, dn)
    across(t, 0)
    greet(0)

    tri = (
        lax.broadcasted_iota(I32, (128, 128), 0) <= lax.broadcasted_iota(I32, (128, 128), 1)
    ).astype(BF16)
    carry = jnp.zeros((32, 1), F32)
    for b in range(rows // 128):
        ids = tenant[:, b * 128:(b + 1) * 128]
        member = (lax.broadcasted_iota(I32, (32, 128), 0) == ids).astype(F32)
        count = carry + jnp.dot(member.astype(BF16), tri, preferred_element_type=F32)
        carry = count[:, 127:128]
        slot = jnp.sum(count * member, axis=0, keepdims=True) - 1.0
        owner = jnp.zeros((1, 128), F32)
        for i in range(n_tenants):
            owner = jnp.where(ids == i, owner_map[i].astype(F32), owner)
        key = owner * float(SLOTS) + slot
        slot_key[:, b * 128:(b + 1) * 128] = key.astype(I32)
        column = jnp.transpose(jnp.broadcast_to(key, (128, 128))).astype(I32)
        slot_hot[b * 128:(b + 1) * 128, :] = (
            column % SLOTS == lax.broadcasted_iota(I32, (128, 128), 1)
        ).astype(BF16)
        row_owner[b * 128:(b + 1) * 128, :] = column // SLOTS

    for j in range(1, nz):
        dz = Z_ORDER[j]
        block = at_tenant(dz, 0)
        wait_block(block)
        if -4 < dz < 0:
            send_block(block, up)
        if 0 < dz < 3:
            send_block(block, dn)
        across(block, j)
        send_u(block)
        relay(j - LAG)
        if j in (2, 4, 6):
            pl.semaphore_wait(token.at[j // 2 - 1], 2)
            if j < 6:
                greet(j // 2)
    for j in range(nz - LAG, nz):
        relay(j)
    for j in range(nz):
        for dx in (1, -1, 2):
            if j < RELAYED and dx == (-1 if j % 2 == 0 else 1):
                continue
            block = at_tenant(Z_ORDER[j], dx)
            wait_block(block)
            send_u(block)

    pick = (
        slot_key[...] == t * SLOTS + lax.broadcasted_iota(I32, (SLOTS, rows), 0)
    ).astype(BF16)
    picked = jnp.dot(pick, g[...], preferred_element_type=F32).astype(BF16)
    part = jnp.transpose(jnp.dot(picked, vq[...], preferred_element_type=F32)).astype(BF16)
    for i in range(n_tensor):
        rank_out[i % NC, i // NC * rank_local:(i // NC + 1) * rank_local, :] = (
            part[i * rank_local:(i + 1) * rank_local, :]
        )
    to_sibling = remote(rank_out.at[1 - c], rank_sib, q_send, q_recv, (t, sibling))
    to_sibling.start()
    to_sibling.wait()
    rank_sum[...] = (rank_out[c].astype(F32) + rank_sib[...].astype(F32)).astype(BF16)

    def ranks_at(i):
        return pl.ds(pl.multiple_of(i * rank_local, rank_local), rank_local)

    for dy in Y_FAR_FIRST:
        to = (y + dy + ny) % ny
        remote(
            rank_sum.at[ranks_at(to)], rank_in.at[ranks_at(y)], r_send, r_recv, (t, at_tensor(dy))
        ).start()
    rank_in[ranks_at(y), :] = rank_sum[ranks_at(y), :]

    step = NC * rows_s

    def shared(i, carry):
        here = pl.ds(pl.multiple_of(i * 2 * step, 2 * step), 2 * step)
        acc[here, :] = jnp.dot(g[here, :], w[...], preferred_element_type=F32)
        return carry

    lax.fori_loop(0, ny // 2, shared, 0)

    wait_bytes(rank_in.at[pl.ds(0, (ny - 1) * rank_local)], r_recv)
    total = jnp.zeros((rank_local, SLOTS), F32)
    for i in range(ny):
        total = total + rank_in[i * rank_local:(i + 1) * rank_local, :].astype(F32)
    code[...] = total.astype(BF16)
    for dz, dx in T_FAR_FIRST:
        remote(code, codes.at[ranks_at(t)], c_send, c_recv, (at_tenant(dz, dx), s)).start()
    codes[ranks_at(t), :] = code[...]
    ur[ranks_at(t), :] = uq[t]

    others = pl.ds(0, (n_tenant - 1) * rank_local)
    wait_bytes(codes.at[others], c_recv)
    wait_bytes(ur.at[others], u_recv)

    owner_lane = lax.broadcasted_iota(I32, (step, n_tenant * rank_local), 1) // rank_local

    def terms(dy):
        d = (y + dy + ny) % ny
        here = pl.ds(pl.multiple_of(d * step, step), step)
        spread_codes = lax.dot_general(
            slot_hot[here, :], codes[...], (((1,), (1,)), ((), ())), preferred_element_type=F32
        )
        owner = row_owner[here, :]
        owner = jnp.concatenate([owner] * (n_tenant * rank_local // 128), axis=1)
        spread_codes = jnp.where(owner == owner_lane, spread_codes, 0.0).astype(BF16)
        acc[here, :] = acc[here, :] + jnp.dot(spread_codes, ur[...], preferred_element_type=F32)
        theirs = pl.ds(pl.multiple_of(d * step + (1 - c) * rows_s, rows_s), rows_s)
        sib_out[d] = acc[theirs, :].astype(BF16)
        remote(sib_out.at[d], sib_in.at[d], x_send, x_recv.at[d], (t, sibling)).start()

    def sibling_ready(dy):
        d = (y + dy + ny) % ny
        wait_bytes(sib_in.at[d], x_recv.at[d])

    pieces = rows_s // PIECE
    low, high = range(pieces // 2), range(pieces // 2, pieces)

    def chip_sum(dy, p):
        d = (y + dy + ny) % ny
        here = pl.ds(pl.multiple_of(d * step + c * rows_s + p * PIECE, PIECE), PIECE)
        return acc[here, :] + sib_in[d, p * PIECE:(p + 1) * PIECE, :].astype(F32)

    def lines(h, p):
        return pl.ds(h * rows_s + p * PIECE, PIECE)

    def ring(way):
        return (ring_up, up_send, up_recv, (t, y_up)) if way > 0 else (
            ring_dn, dn_send, dn_recv, (t, y_dn)
        )

    def push(way, source, h, p):
        slots, send, recv, to = ring(way)
        remote(source, slots.at[lines(h, p)], send, recv.at[h, p], to).start()

    def fresh(way, p):
        slots = ring(way)[0]
        slots[lines(0, p), :] = chip_sum(3 * way, p).astype(BF16)
        push(way, slots.at[lines(0, p)], 1, p)

    def arrived(way, h, p):
        slots, send, recv, to = ring(way)
        wait_bytes(slots.at[lines(h, p)], recv.at[h, p])
        return slots[lines(h, p), :].astype(F32)

    def forward(way, h, p):
        slots = ring(way)[0]
        slots[lines(h, p), :] = (arrived(way, h, p) + chip_sum((3 - h) * way, p)).astype(BF16)
        push(way, slots.at[lines(h, p)], h + 1, p)

    terms(4)
    terms(3)
    sibling_ready(4)
    for p in range(pieces):
        stage[p * PIECE:(p + 1) * PIECE, :] = chip_sum(4, p).astype(BF16)
        push(1 if p in low else -1, stage.at[pl.ds(p * PIECE, PIECE)], 0, p)
    terms(-3)
    sibling_ready(3)
    for p in high:
        fresh(1, p)
    terms(2)
    sibling_ready(-3)
    for p in low:
        fresh(-1, p)
    terms(-2)
    terms(1)
    for p in range(pieces // 2):
        forward(1, 0, low[p])
        forward(-1, 0, high[p])
    terms(-1)
    sibling_ready(2)
    sibling_ready(-2)
    for p in range(pieces):
        forward(1, 1, (p + pieces // 2) % pieces)
        forward(-1, 1, p)
    terms(0)
    sibling_ready(1)
    sibling_ready(-1)
    for p in range(pieces):
        forward(1, 2, (p + pieces // 2) % pieces)
        forward(-1, 2, p)
    sibling_ready(0)
    for i in range(pieces):
        p = (i // 2 + (i % 2) * (pieces // 2)) % pieces
        out[p * PIECE:(p + 1) * PIECE, :] = (
            arrived(1, 3, p) + arrived(-1, 3, p) + chip_sum(0, p)
        ).astype(BF16)

    wait_bytes(g.at[pl.ds(0, (n_tenant - 1) * rows_t)], a_send)
    wait_bytes(ur.at[others], u_send)
    wait_bytes(rank_in.at[pl.ds(0, (ny - 1) * rank_local)], r_send)
    wait_bytes(codes.at[others], c_send)
    wait_bytes(sib_out, x_send)
    wait_bytes(ring_up.at[pl.ds(0, 3 * rows_s + rows_s // 2)], up_send)
    wait_bytes(ring_dn.at[pl.ds(0, 3 * rows_s + rows_s // 2)], dn_send)


def on_device(
    n_tenant, n_tensor,
    activations, base_weight, v_codes, u_codes, group_bits, v_scale, u_scale, tenant_of, owner_map,
):
    rows_t, depth = activations.shape
    cols = base_weight.shape[1]
    rows = tenant_of.shape[0]
    full_rank = v_codes.shape[2]
    rank_local = u_codes.shape[1]
    rows_s = rows // n_tensor
    ny = n_tensor // NC
    all_ranks = n_tenant * rank_local
    vmem = pl.BlockSpec(memory_space=pltpu.VMEM)
    smem = pl.BlockSpec(memory_space=pltpu.SMEM)
    hbm = pl.BlockSpec(memory_space=pl.ANY)
    dma = pltpu.SemaphoreType.DMA
    pieces = rows_s // PIECE
    return pl.pallas_call(
        functools.partial(kernel, n_tenant=n_tenant, n_tensor=n_tensor),
        out_shape=jax.ShapeDtypeStruct((rows_s, cols), BF16),
        in_specs=[hbm, hbm, hbm, hbm, smem, vmem, vmem, vmem, smem],
        out_specs=vmem,
        scratch_shapes=[
            pltpu.VMEM((rows, depth), BF16),
            pltpu.VMEM((depth, cols), BF16),
            pltpu.VMEM((depth, full_rank), I32),
            pltpu.VMEM(u_codes.shape[1:], I32),
            pltpu.VMEM((n_tenant, rank_local, cols), BF16),
            pltpu.VMEM((depth, full_rank), BF16),
            pltpu.VMEM((all_ranks, cols), BF16),
            pltpu.VMEM((NC, full_rank // NC, SLOTS), BF16),
            pltpu.VMEM((full_rank // NC, SLOTS), BF16),
            pltpu.VMEM((full_rank // NC, SLOTS), BF16),
            pltpu.VMEM((full_rank // NC, SLOTS), BF16),
            pltpu.VMEM((rank_local, SLOTS), BF16),
            pltpu.VMEM((all_ranks, SLOTS), BF16),
            pltpu.VMEM((rows, SLOTS), BF16),
            pltpu.VMEM((rows, 128), I32),
            pltpu.VMEM((1, rows), I32),
            pltpu.VMEM((rows, cols), F32),
            pltpu.VMEM((ny, rows_s, cols), BF16),
            pltpu.VMEM((ny, rows_s, cols), BF16),
            pltpu.VMEM((rows_s, cols), BF16),
            pltpu.VMEM((4 * rows_s, cols), BF16),
            pltpu.VMEM((4 * rows_s, cols), BF16),
            dma((4,)), dma, dma((n_tenant,)), dma, dma, dma, dma, dma, dma, dma, dma,
            dma, dma((ny,)), dma, dma((4, pieces)), dma, dma((4, pieces)),
            pltpu.SemaphoreType.REGULAR((3,)),
        ],
        compiler_params=pltpu.CompilerParams(
            collective_id=0, has_side_effects=True, vmem_limit_bytes=58 * 1024 * 1024
        ),
        name="up_projection",
    )(
        activations, base_weight, v_codes, u_codes, group_bits, v_scale, u_scale,
        tenant_of.reshape(1, rows), owner_map,
    )


def solution(mesh):
    in_specs = (
        P("tenant", "tensor"),
        P("tensor", "tenant"),
        P("tenant", "tensor", None),
        P("tenant", "tensor", None),
        P("tenant", None),
        P("tenant", None),
        P("tenant", "tensor"),
        P(),
        P(),
    )
    return jax.shard_map(
        functools.partial(on_device, mesh.shape["tenant"], mesh.shape["tensor"]),
        mesh=mesh, in_specs=in_specs, out_specs=P("tensor", "tenant"), check_vma=False,
    )
```

```python
import functools
from typing import Any, NamedTuple

import jax
import jax.numpy as jnp
from jax import lax
from jax.experimental import pallas as pl
from jax.experimental.pallas import tpu as pltpu
from jax.sharding import PartitionSpec as P

MESH = pl.DeviceIdType.MESH
BF16, F32, I32 = jnp.bfloat16, jnp.float32, jnp.int32

NX, NC = 4, 2
SLOTS = 128
Z_ORDER = (0, -1, 1, -2, 2, -3, 3, -4)
RELAYED = 6
PLANES_AFTER = ((), (), (), (), (1, -1, 2, -2), (3, -3, 4), (), ())
SPREAD_FIRST = (0,1,-1)
SPREAD_EARLY, SPREAD_LATE = (2,-2,3,-3),(4,)
LAG = 3
PIECE = 48
STRAIGHT_EARLY = 12
PART_ORDER = (0,2,1,0,1,0,1,0,1,0,1)
Y_FAR_FIRST = (4, 3, -3, 2, -2, 1, -1)
T_MIXED = tuple(
    ((0, 4, 1, -1, 3, -3, 2, -2)[i * 3 % 8], (0, 2, 1, -1)[(i + i // 8) % 4]) for i in range(1, 32)
)
T_FAR_FIRST = tuple(
    sorted(
        ((dz, dx) for dz in Z_ORDER for dx in (0, 1, -1, 2) if (dz, dx) != (0, 0)),
        key=lambda at: -abs(at[0]) - abs(at[1]),
    )
)


class Part(NamedTuple):
    uq: Any
    ur: Any
    sib_out: Any
    sib_in: Any
    stage: Any
    ring_up: Any
    ring_dn: Any
    u_send: Any
    u_recv: Any
    x_send: Any
    x_recv: Any
    up_send: Any
    up_recv: Any
    dn_send: Any
    dn_recv: Any


def kernel(
    act, w_hbm, vc_hbm, uc_hbm, bits, v_scale, u_scale, tenant, owner_map, out,
    g, w, vc, uc, vq, rank_out, rank_sib, rank_sum, rank_in, code, codes,
    slot_hot, row_owner, slot_key, mixed, acc, uz,
    load_sem, a_send, a_recv, uz_send, uz_recv, q_send, q_recv, r_send, r_recv, c_send, c_recv,
    token, *parts, n_tenant, n_tensor, widths,
):
    parts = [Part(*parts[i::len(widths)]) for i in range(len(widths))]
    starts = [sum(widths[:i]) for i in range(len(widths))]
    first, second = parts
    t, s = lax.axis_index("tenant"), lax.axis_index("tensor")
    nz, ny = n_tenant // NX, n_tensor // NC
    z, x = t // NX, t % NX
    y, c = s // NC, s % NC
    rows_t, depth = act.shape
    rows = g.shape[0]
    cols = w.shape[1]
    rank_local = uc.shape[0]
    full_rank = vc.shape[1]
    n_tenants = owner_map.shape[0]
    group = full_rank // bits.shape[1]
    rows_s = out.shape[0]

    def remote(src, dst, send_sem, recv_sem, device):
        return pltpu.make_async_remote_copy(
            src_ref=src, dst_ref=dst, send_sem=send_sem, recv_sem=recv_sem,
            device_id=device, device_id_type=MESH,
        )

    def wait_bytes(ref, sem):
        pltpu.make_async_copy(ref, ref, sem).wait()

    def at_tenant(dz, dx):
        return ((z + dz + nz) % nz) * NX + (x + dx + NX) % NX

    def at_tensor(dy):
        return ((y + dy + ny) % ny) * NC + c

    up, dn, right, left = at_tenant(1, 0), at_tenant(-1, 0), at_tenant(0, 1), at_tenant(0, -1)
    y_up, y_dn, sibling = at_tensor(1), at_tensor(-1), y * NC + 1 - c

    loads = [
        pltpu.make_async_copy(uc_hbm.at[0], uc, load_sem.at[0]),
        pltpu.make_async_copy(vc_hbm.at[0], vc, load_sem.at[1]),
        pltpu.make_async_copy(w_hbm, w, load_sem.at[2]),
        pltpu.make_async_copy(act, g.at[pl.ds(t * rows_t, rows_t)], load_sem.at[3]),
    ]
    for load in loads:
        load.start()

    barrier = pltpu.get_barrier_semaphore()
    for device in (
        (up, s), (dn, s), (at_tenant(2, 0), s), (at_tenant(-2, 0), s),
        (right, s), (left, s), (t, y_up), (t, y_dn), (t, sibling),
    ):
        pl.semaphore_signal(barrier, 1, device_id=device, device_id_type=MESH)

    pl.semaphore_wait(barrier, 9)

    def g_at(block):
        return g.at[pl.ds(block * rows_t, rows_t)]

    def send_block(block, to):
        remote(g_at(block), g_at(block), a_send, a_recv.at[block], (to, s)).start()

    def wait_block(block):
        wait_bytes(g_at(block), a_recv.at[block])

    def send_planes(dz):
        there = (z + dz + nz) % nz
        remote(
            first.uq.at[pl.ds(there * NX, NX)], uz.at[z], uz_send, uz_recv.at[z], (at_tenant(dz, 0), s)
        ).start()

    def hand_on(dz):
        plane = (z + dz + nz) % nz
        source = uz.at[plane] if dz else first.uq.at[pl.ds(z * NX, NX)]
        if dz:
            wait_bytes(source, uz_recv.at[plane])
        here = ranks_at(plane * NX + x)
        for dx in (2, 1, -1):
            there = (x + dx + NX) % NX
            remote(
                source.at[there], first.ur.at[here], first.u_send, first.u_recv,
                (at_tenant(0, dx), s),
            ).start()
        first.ur[here, :] = source[x]

    def send_columns(dz, dx):
        there = at_tenant(dz, dx)
        remote(
            second.uq.at[there], second.ur.at[ranks_at(t)], second.u_send, second.u_recv,
            (there, s),
        ).start()

    def ranks_at(i):
        return pl.ds(pl.multiple_of(i * rank_local, rank_local), rank_local)

    def across(block, j):
        send_block(block, right)
        send_block(block, left)
        if j >= RELAYED:
            send_block(block, at_tenant(0, 2))

    def relay(j):
        if 0 <= j < RELAYED:
            block = at_tenant(Z_ORDER[j], -1 if j % 2 == 0 else 1)
            wait_block(block)
            send_block(block, right if j % 2 == 0 else left)

    def greet(i):
        for device in ((t, y_up), (t, y_dn)):
            pl.semaphore_signal(token.at[i], 1, device_id=device, device_id_type=MESH)

    for to in (up, dn, at_tenant(2, 0), at_tenant(-2, 0), right, left):
        remote(act, g_at(t), a_send, a_recv.at[t], (to, s)).start()
    greet(0)

    u_spread = (jnp.left_shift(1, bits[0, s * rank_local // group]) - 1).astype(F32)
    diagonal = lax.broadcasted_iota(I32, (rank_local, rank_local), 0) == lax.broadcasted_iota(
        I32, (rank_local, rank_local), 1
    )
    u_factor = (
        jnp.sum(jnp.where(diagonal, u_scale[...], 0.0), axis=1, keepdims=True) / u_spread
    )
    loads[0].wait()

    def dequantize_u(i, carry):
        for part, start, width in zip(parts, starts, widths):
            block = uc[:, pl.ds(pl.multiple_of(i * cols + start, 128), width)]
            part.uq[i] = ((2.0 * block.astype(F32) - u_spread) * u_factor).astype(BF16)
        return carry

    lax.fori_loop(0, n_tenant, dequantize_u, 0)

    lane = lax.broadcasted_iota(I32, (1, full_rank), 1)
    v_spread = jnp.zeros((1, full_rank), F32)
    for i in range(bits.shape[1]):
        spread = (jnp.left_shift(1, bits[0, i]) - 1).astype(F32)
        v_spread = jnp.where(lane // group == i, spread, v_spread)
    v_factor = v_scale[...] / v_spread
    loads[1].wait()
    vq[...] = ((2.0 * vc[...].astype(F32) - v_spread) * v_factor).astype(BF16)

    tri = (
        lax.broadcasted_iota(I32, (128, 128), 0) <= lax.broadcasted_iota(I32, (128, 128), 1)
    ).astype(BF16)
    carry = jnp.zeros((32, 1), F32)
    for b in range(rows // 128):
        ids = tenant[:, b * 128:(b + 1) * 128]
        member = (lax.broadcasted_iota(I32, (32, 128), 0) == ids).astype(F32)
        count = carry + jnp.dot(member.astype(BF16), tri, preferred_element_type=F32)
        carry = count[:, 127:128]
        slot = jnp.sum(count * member, axis=0, keepdims=True) - 1.0
        owner = jnp.zeros((1, 128), F32)
        for i in range(n_tenants):
            owner = jnp.where(ids == i, owner_map[i].astype(F32), owner)
        key = owner * float(SLOTS) + slot
        slot_key[:, b * 128:(b + 1) * 128] = key.astype(I32)
        column = jnp.transpose(jnp.broadcast_to(key, (128, 128))).astype(I32)
        slot_hot[b * 128:(b + 1) * 128, :] = (
            column % SLOTS == lax.broadcasted_iota(I32, (128, 128), 1)
        ).astype(BF16)
        row_owner[b * 128:(b + 1) * 128, :] = column // SLOTS

    for j in range(1, nz):
        dz = Z_ORDER[j]
        block = at_tenant(dz, 0)
        wait_block(block)
        if dz == -2:
            send_block(block, up)
            send_block(block, at_tenant(2, 0))
        if dz == 2:
            send_block(block, dn)
        across(block, j)
        relay(j - LAG)
        if j in (2, 4, 6):
            pl.semaphore_wait(token.at[j // 2 - 1], 2)
            if j < 6:
                greet(j // 2)
        for dz in PLANES_AFTER[j]:
            send_planes(dz)
    for j in range(nz - LAG, nz):
        relay(j)
    for j in range(nz):
        for dx in (1, -1, 2):
            if j < RELAYED and dx == (-1 if j % 2 == 0 else 1):
                continue
            block = at_tenant(Z_ORDER[j], dx)
            wait_block(block)
    loads[2].wait()
    loads[3].wait()

    pick = (
        slot_key[...] == t * SLOTS + lax.broadcasted_iota(I32, (SLOTS, rows), 0)
    ).astype(BF16)
    picked = jnp.dot(pick, g[...], preferred_element_type=F32).astype(BF16)
    part = jnp.transpose(jnp.dot(picked, vq[...], preferred_element_type=F32)).astype(BF16)
    for i in range(n_tensor):
        rank_out[i % NC, i // NC * rank_local:(i // NC + 1) * rank_local, :] = (
            part[i * rank_local:(i + 1) * rank_local, :]
        )
    to_sibling = remote(rank_out.at[1 - c], rank_sib, q_send, q_recv, (t, sibling))
    to_sibling.start()
    to_sibling.wait()
    rank_sum[...] = (rank_out[c].astype(F32) + rank_sib[...].astype(F32)).astype(BF16)

    for dy in Y_FAR_FIRST:
        to = (y + dy + ny) % ny
        remote(
            rank_sum.at[ranks_at(to)], rank_in.at[ranks_at(y)], r_send, r_recv, (t, at_tensor(dy))
        ).start()
    rank_in[ranks_at(y), :] = rank_sum[ranks_at(y), :]

    for dz in SPREAD_FIRST:
        hand_on(dz)
    for dz, dx in T_MIXED[:STRAIGHT_EARLY]:
        send_columns(dz, dx)
    step = NC * rows_s

    def shared(i, carry):
        here = pl.ds(pl.multiple_of(i * 2 * step, 2 * step), 2 * step)
        acc[here, :] = jnp.dot(g[here, :], w[...], preferred_element_type=F32)
        return carry

    lax.fori_loop(0, ny // 2, shared, 0)

    for dz in SPREAD_EARLY:
        hand_on(dz)
    wait_bytes(rank_in.at[pl.ds(0, (ny - 1) * rank_local)], r_recv)
    total = jnp.zeros((rank_local, SLOTS), F32)
    for i in range(ny):
        total = total + rank_in[i * rank_local:(i + 1) * rank_local, :].astype(F32)
    code[...] = total.astype(BF16)
    for dz, dx in T_FAR_FIRST:
        remote(code, codes.at[ranks_at(t)], c_send, c_recv, (at_tenant(dz, dx), s)).start()
    codes[ranks_at(t), :] = code[...]
    for dz in SPREAD_LATE:
        hand_on(dz)
    for dz, dx in T_MIXED[STRAIGHT_EARLY:]:
        send_columns(dz, dx)
    second.ur[ranks_at(t), :] = second.uq[t]

    others = pl.ds(0, (n_tenant - 1) * rank_local)
    wait_bytes(codes.at[others], c_recv)
    wait_bytes(first.ur.at[pl.ds(0, nz * (NX - 1) * rank_local)], first.u_recv)

    owner_lane = lax.broadcasted_iota(I32, (step, n_tenant * rank_local), 1) // rank_local

    def mix(dy):
        d = (y + dy + ny) % ny
        here = pl.ds(pl.multiple_of(d * step, step), step)
        spread_codes = lax.dot_general(
            slot_hot[here, :], codes[...], (((1,), (1,)), ((), ())), preferred_element_type=F32
        )
        owner = row_owner[here, :]
        owner = jnp.concatenate([owner] * (n_tenant * rank_local // 128), axis=1)
        mixed[here, :] = jnp.where(owner == owner_lane, spread_codes, 0.0).astype(BF16)

    pieces = rows_s // PIECE
    low, high = range(pieces // 2), range(pieces // 2, pieces)

    def reduce_part(part, start, width):
        span = slice(start, start + width)

        def terms(dy):
            d = (y + dy + ny) % ny
            here = pl.ds(pl.multiple_of(d * step, step), step)
            if part is first:
                mix(dy)
            acc[here, span] = acc[here, span] + jnp.dot(
                mixed[here, :], part.ur[...], preferred_element_type=F32
            )
            theirs = pl.ds(pl.multiple_of(d * step + (1 - c) * rows_s, rows_s), rows_s)
            part.sib_out[d] = acc[theirs, span].astype(BF16)
            remote(
                part.sib_out.at[d], part.sib_in.at[d], part.x_send, part.x_recv.at[d], (t, sibling)
            ).start()

        def sibling_ready(dy):
            d = (y + dy + ny) % ny
            wait_bytes(part.sib_in.at[d], part.x_recv.at[d])

        def chip_sum(dy, p):
            d = (y + dy + ny) % ny
            here = pl.ds(pl.multiple_of(d * step + c * rows_s + p * PIECE, PIECE), PIECE)
            return acc[here, span] + part.sib_in[d, p * PIECE:(p + 1) * PIECE, :].astype(F32)

        def lines(h, p):
            return pl.ds(h * rows_s + p * PIECE, PIECE)

        def ring(way):
            return (part.ring_up, part.up_send, part.up_recv, (t, y_up)) if way > 0 else (
                part.ring_dn, part.dn_send, part.dn_recv, (t, y_dn)
            )

        def push(way, source, h, p):
            slots, send, recv, to = ring(way)
            remote(source, slots.at[lines(h, p)], send, recv.at[h, p], to).start()

        def fresh(way, p):
            slots = ring(way)[0]
            slots[lines(0, p), :] = chip_sum(3 * way, p).astype(BF16)
            push(way, slots.at[lines(0, p)], 1, p)

        def arrived(way, h, p):
            slots, send, recv, to = ring(way)
            wait_bytes(slots.at[lines(h, p)], recv.at[h, p])
            return slots[lines(h, p), :].astype(F32)

        def forward(way, h, p):
            slots = ring(way)[0]
            slots[lines(h, p), :] = (arrived(way, h, p) + chip_sum((3 - h) * way, p)).astype(BF16)
            push(way, slots.at[lines(h, p)], h + 1, p)

        terms(4)
        terms(3)
        sibling_ready(4)
        for p in range(pieces):
            part.stage[p * PIECE:(p + 1) * PIECE, :] = chip_sum(4, p).astype(BF16)
            push(1 if p in low else -1, part.stage.at[pl.ds(p * PIECE, PIECE)], 0, p)
        terms(-3)
        sibling_ready(3)
        for p in high:
            fresh(1, p)
        terms(2)
        sibling_ready(-3)
        for p in low:
            fresh(-1, p)
        terms(-2)
        terms(1)
        yield
        for p in range(pieces // 2):
            forward(1, 0, low[p])
            forward(-1, 0, high[p])
        terms(-1)
        sibling_ready(2)
        sibling_ready(-2)
        yield
        for p in range(pieces):
            forward(1, 1, (p + pieces // 2) % pieces)
            forward(-1, 1, p)
        terms(0)
        sibling_ready(1)
        sibling_ready(-1)
        yield
        for p in range(pieces):
            forward(1, 2, (p + pieces // 2) % pieces)
            forward(-1, 2, p)
        sibling_ready(0)
        yield
        for i in range(pieces):
            p = (i // 2 + (i % 2) * (pieces // 2)) % pieces
            out[p * PIECE:(p + 1) * PIECE, span] = (
                arrived(1, 3, p) + arrived(-1, 3, p) + chip_sum(0, p)
            ).astype(BF16)
        yield

    sums = [reduce_part(*each) for each in zip(parts, starts, widths)]
    for which in PART_ORDER:
        if which == 2:
            wait_bytes(second.ur.at[others], second.u_recv)
            continue
        next(sums[which])

    wait_bytes(g.at[pl.ds(0, (n_tenant - 1) * rows_t)], a_send)
    wait_bytes(uz.at[pl.ds(0, nz - 1)], uz_send)
    wait_bytes(first.ur.at[pl.ds(0, nz * (NX - 1) * rank_local)], first.u_send)
    wait_bytes(second.ur.at[others], second.u_send)
    wait_bytes(rank_in.at[pl.ds(0, (ny - 1) * rank_local)], r_send)
    wait_bytes(codes.at[others], c_send)
    for part in parts:
        wait_bytes(part.sib_out, part.x_send)
        wait_bytes(part.ring_up.at[pl.ds(0, 3 * rows_s + rows_s // 2)], part.up_send)
        wait_bytes(part.ring_dn.at[pl.ds(0, 3 * rows_s + rows_s // 2)], part.dn_send)


def on_device(
    n_tenant, n_tensor,
    activations, base_weight, v_codes, u_codes, group_bits, v_scale, u_scale, tenant_of, owner_map,
):
    rows_t, depth = activations.shape
    cols = base_weight.shape[1]
    rows = tenant_of.shape[0]
    full_rank = v_codes.shape[2]
    rank_local = u_codes.shape[1]
    rows_s = rows // n_tensor
    ny = n_tensor // NC
    all_ranks = n_tenant * rank_local
    vmem = pl.BlockSpec(memory_space=pltpu.VMEM)
    smem = pl.BlockSpec(memory_space=pltpu.SMEM)
    hbm = pl.BlockSpec(memory_space=pl.ANY)
    dma = pltpu.SemaphoreType.DMA
    pieces = rows_s // PIECE
    widths = (cols // 256 * 128 + 128, cols - cols // 256 * 128 - 128)
    return pl.pallas_call(
        functools.partial(kernel, n_tenant=n_tenant, n_tensor=n_tensor, widths=widths),
        out_shape=jax.ShapeDtypeStruct((rows_s, cols), BF16),
        in_specs=[hbm, hbm, hbm, hbm, smem, vmem, vmem, vmem, smem],
        out_specs=vmem,
        scratch_shapes=[
            pltpu.VMEM((rows, depth), BF16),
            pltpu.VMEM((depth, cols), BF16),
            pltpu.VMEM((depth, full_rank), I32),
            pltpu.VMEM(u_codes.shape[1:], I32),
            pltpu.VMEM((depth, full_rank), BF16),
            pltpu.VMEM((NC, full_rank // NC, SLOTS), BF16),
            pltpu.VMEM((full_rank // NC, SLOTS), BF16),
            pltpu.VMEM((full_rank // NC, SLOTS), BF16),
            pltpu.VMEM((full_rank // NC, SLOTS), BF16),
            pltpu.VMEM((rank_local, SLOTS), BF16),
            pltpu.VMEM((all_ranks, SLOTS), BF16),
            pltpu.VMEM((rows, SLOTS), BF16),
            pltpu.VMEM((rows, 128), I32),
            pltpu.VMEM((1, rows), I32),
            pltpu.VMEM((rows, all_ranks), BF16),
            pltpu.VMEM((rows, cols), F32),
            pltpu.VMEM((n_tenant // NX, NX, rank_local, widths[0]), BF16),
            dma((4,)), dma, dma((n_tenant,)), dma, dma((n_tenant // NX,)), dma, dma, dma, dma,
            dma, dma, pltpu.SemaphoreType.REGULAR((3,)),
            *[pltpu.VMEM((n_tenant, rank_local, width), BF16) for width in widths],
            *[pltpu.VMEM((all_ranks, width), BF16) for width in widths],
            *[pltpu.VMEM((ny, rows_s, width), BF16) for width in widths],
            *[pltpu.VMEM((ny, rows_s, width), BF16) for width in widths],
            *[pltpu.VMEM((rows_s, width), BF16) for width in widths],
            *[pltpu.VMEM((4 * rows_s, width), BF16) for width in widths],
            *[pltpu.VMEM((4 * rows_s, width), BF16) for width in widths],
            dma, dma, dma, dma, dma, dma, dma((ny,)), dma((ny,)),
            dma, dma, dma((4, pieces)), dma((4, pieces)),
            dma, dma, dma((4, pieces)), dma((4, pieces)),
        ],
        compiler_params=pltpu.CompilerParams(
            collective_id=0, has_side_effects=True, vmem_limit_bytes=58 * 1024 * 1024
        ),
        name="up_projection",
    )(
        activations, base_weight, v_codes, u_codes, group_bits, v_scale, u_scale,
        tenant_of.reshape(1, rows), owner_map,
    )


def solution(mesh):
    in_specs = (
        P("tenant", "tensor"),
        P("tensor", "tenant"),
        P("tenant", "tensor", None),
        P("tenant", "tensor", None),
        P("tenant", None),
        P("tenant", None),
        P("tenant", "tensor"),
        P(),
        P(),
    )
    return jax.shard_map(
        functools.partial(on_device, mesh.shape["tenant"], mesh.shape["tensor"]),
        mesh=mesh, in_specs=in_specs, out_specs=P("tensor", "tenant"), check_vma=False,
    )
```

```python
import functools
from typing import Any, NamedTuple

import jax
import jax.numpy as jnp
from jax import lax
from jax.experimental import pallas as pl
from jax.experimental.pallas import tpu as pltpu
from jax.sharding import PartitionSpec as P

MESH = pl.DeviceIdType.MESH
BF16, F32, I32 = jnp.bfloat16, jnp.float32, jnp.int32

NX, NC = 4, 2
SLOTS = 128
Z_ORDER = (0, -1, 1, -2, 2, -3, 3, -4)
RELAYED = 6
PLANES_AFTER = ((), (), (), (), (1, -1, 2, -2), (3, -3, 4), (), ())
SPREAD_FIRST = (0,1,-1)
SPREAD_EARLY, SPREAD_LATE = (2,-2,3,-3),(4,)
LAG = 3
MIXED_FIRST = (4, 3, -3, 2)
PIECE = 48
STRAIGHT_EARLY = 12
PART_ORDER = (0,2,1,0,1,0,1,0,1,0,1)
Y_FAR_FIRST = (4, 3, -3, 2, -2, 1, -1)
T_MIXED = tuple(
    ((0, 4, 1, -1, 3, -3, 2, -2)[i * 3 % 8], (0, 2, 1, -1)[(i + i // 8) % 4]) for i in range(1, 32)
)
T_FAR_FIRST = tuple(
    sorted(
        ((dz, dx) for dz in Z_ORDER for dx in (0, 1, -1, 2) if (dz, dx) != (0, 0)),
        key=lambda at: -abs(at[0]) - abs(at[1]),
    )
)


class Part(NamedTuple):
    uq: Any
    ur: Any
    sib_out: Any
    sib_in: Any
    stage: Any
    ring_up: Any
    ring_dn: Any
    u_send: Any
    u_recv: Any
    x_send: Any
    x_recv: Any
    up_send: Any
    up_recv: Any
    dn_send: Any
    dn_recv: Any


def kernel(
    act, w_hbm, vc_hbm, uc_hbm, bits, v_scale, u_scale, tenant, owner_map, out,
    g, w, vc, uc, vq, rank_out, rank_sib, rank_sum, rank_in, code, codes,
    slot_hot, row_owner, slot_key, mixed, acc, uz,
    load_sem, a_send, a_recv, uz_send, uz_recv, q_send, q_recv, r_send, r_recv, c_send, c_recv,
    token, *parts, n_tenant, n_tensor, widths,
):
    parts = [Part(*parts[i::len(widths)]) for i in range(len(widths))]
    starts = [sum(widths[:i]) for i in range(len(widths))]
    first, second = parts
    t, s = lax.axis_index("tenant"), lax.axis_index("tensor")
    nz, ny = n_tenant // NX, n_tensor // NC
    z, x = t // NX, t % NX
    y, c = s // NC, s % NC
    rows_t, depth = act.shape
    rows = g.shape[0]
    cols = w.shape[1]
    rank_local = uc.shape[0]
    full_rank = vc.shape[1]
    n_tenants = owner_map.shape[0]
    group = full_rank // bits.shape[1]
    rows_s = out.shape[0]

    def remote(src, dst, send_sem, recv_sem, device):
        return pltpu.make_async_remote_copy(
            src_ref=src, dst_ref=dst, send_sem=send_sem, recv_sem=recv_sem,
            device_id=device, device_id_type=MESH,
        )

    def wait_bytes(ref, sem):
        pltpu.make_async_copy(ref, ref, sem).wait()

    def at_tenant(dz, dx):
        return ((z + dz + nz) % nz) * NX + (x + dx + NX) % NX

    def at_tensor(dy):
        return ((y + dy + ny) % ny) * NC + c

    up, dn, right, left = at_tenant(1, 0), at_tenant(-1, 0), at_tenant(0, 1), at_tenant(0, -1)
    y_up, y_dn, sibling = at_tensor(1), at_tensor(-1), y * NC + 1 - c

    loads = [
        pltpu.make_async_copy(uc_hbm.at[0], uc, load_sem.at[0]),
        pltpu.make_async_copy(vc_hbm.at[0], vc, load_sem.at[1]),
        pltpu.make_async_copy(w_hbm, w, load_sem.at[2]),
        pltpu.make_async_copy(act, g.at[pl.ds(t * rows_t, rows_t)], load_sem.at[3]),
    ]
    for load in loads:
        load.start()

    barrier = pltpu.get_barrier_semaphore()
    for device in (
        (up, s), (dn, s), (at_tenant(2, 0), s), (at_tenant(-2, 0), s),
        (right, s), (left, s), (t, y_up), (t, y_dn), (t, sibling),
    ):
        pl.semaphore_signal(barrier, 1, device_id=device, device_id_type=MESH)

    pl.semaphore_wait(barrier, 9)

    def g_at(block):
        return g.at[pl.ds(block * rows_t, rows_t)]

    def send_block(block, to):
        remote(g_at(block), g_at(block), a_send, a_recv.at[block], (to, s)).start()

    def wait_block(block):
        wait_bytes(g_at(block), a_recv.at[block])

    def send_planes(dz):
        there = (z + dz + nz) % nz
        remote(
            first.uq.at[pl.ds(there * NX, NX)], uz.at[z], uz_send, uz_recv.at[z], (at_tenant(dz, 0), s)
        ).start()

    def hand_on(dz):
        plane = (z + dz + nz) % nz
        source = uz.at[plane] if dz else first.uq.at[pl.ds(z * NX, NX)]
        if dz:
            wait_bytes(source, uz_recv.at[plane])
        here = ranks_at(plane * NX + x)
        for dx in (2, 1, -1):
            there = (x + dx + NX) % NX
            remote(
                source.at[there], first.ur.at[here], first.u_send, first.u_recv,
                (at_tenant(0, dx), s),
            ).start()
        first.ur[here, :] = source[x]

    def send_columns(dz, dx):
        there = at_tenant(dz, dx)
        remote(
            second.uq.at[there], second.ur.at[ranks_at(t)], second.u_send, second.u_recv,
            (there, s),
        ).start()

    def ranks_at(i):
        return pl.ds(pl.multiple_of(i * rank_local, rank_local), rank_local)

    def across(block, j):
        send_block(block, right)
        send_block(block, left)
        if j >= RELAYED:
            send_block(block, at_tenant(0, 2))

    def relay(j):
        if 0 <= j < RELAYED:
            block = at_tenant(Z_ORDER[j], -1 if j % 2 == 0 else 1)
            wait_block(block)
            send_block(block, right if j % 2 == 0 else left)

    def greet(i):
        for device in ((t, y_up), (t, y_dn)):
            pl.semaphore_signal(token.at[i], 1, device_id=device, device_id_type=MESH)

    for to in (up, dn, at_tenant(2, 0), at_tenant(-2, 0), right, left):
        remote(act, g_at(t), a_send, a_recv.at[t], (to, s)).start()
    greet(0)

    u_spread = (jnp.left_shift(1, bits[0, s * rank_local // group]) - 1).astype(F32)
    diagonal = lax.broadcasted_iota(I32, (rank_local, rank_local), 0) == lax.broadcasted_iota(
        I32, (rank_local, rank_local), 1
    )
    u_factor = (
        jnp.sum(jnp.where(diagonal, u_scale[...], 0.0), axis=1, keepdims=True) / u_spread
    )
    loads[0].wait()

    def dequantize_u(i, carry):
        for part, start, width in zip(parts, starts, widths):
            block = uc[:, pl.ds(pl.multiple_of(i * cols + start, 128), width)]
            part.uq[i] = ((2.0 * block.astype(F32) - u_spread) * u_factor).astype(BF16)
        return carry

    lax.fori_loop(0, n_tenant, dequantize_u, 0)

    lane = lax.broadcasted_iota(I32, (1, full_rank), 1)
    v_spread = jnp.zeros((1, full_rank), F32)
    for i in range(bits.shape[1]):
        spread = (jnp.left_shift(1, bits[0, i]) - 1).astype(F32)
        v_spread = jnp.where(lane // group == i, spread, v_spread)
    v_factor = v_scale[...] / v_spread
    loads[1].wait()
    vq[...] = ((2.0 * vc[...].astype(F32) - v_spread) * v_factor).astype(BF16)

    tri = (
        lax.broadcasted_iota(I32, (128, 128), 0) <= lax.broadcasted_iota(I32, (128, 128), 1)
    ).astype(BF16)
    carry = jnp.zeros((32, 1), F32)
    for b in range(rows // 128):
        ids = tenant[:, b * 128:(b + 1) * 128]
        member = (lax.broadcasted_iota(I32, (32, 128), 0) == ids).astype(F32)
        count = carry + jnp.dot(member.astype(BF16), tri, preferred_element_type=F32)
        carry = count[:, 127:128]
        slot = jnp.sum(count * member, axis=0, keepdims=True) - 1.0
        owner = jnp.zeros((1, 128), F32)
        for i in range(n_tenants):
            owner = jnp.where(ids == i, owner_map[i].astype(F32), owner)
        key = owner * float(SLOTS) + slot
        slot_key[:, b * 128:(b + 1) * 128] = key.astype(I32)
        column = jnp.transpose(jnp.broadcast_to(key, (128, 128))).astype(I32)
        slot_hot[b * 128:(b + 1) * 128, :] = (
            column % SLOTS == lax.broadcasted_iota(I32, (128, 128), 1)
        ).astype(BF16)
        row_owner[b * 128:(b + 1) * 128, :] = column // SLOTS

    for j in range(1, nz):
        dz = Z_ORDER[j]
        block = at_tenant(dz, 0)
        wait_block(block)
        if dz == -2:
            send_block(block, up)
            send_block(block, at_tenant(2, 0))
        if dz == 2:
            send_block(block, dn)
        across(block, j)
        relay(j - LAG)
        if j in (2, 4, 6):
            pl.semaphore_wait(token.at[j // 2 - 1], 2)
            if j < 6:
                greet(j // 2)
        for dz in PLANES_AFTER[j]:
            send_planes(dz)
    for j in range(nz - LAG, nz):
        relay(j)
    for j in range(nz):
        for dx in (1, -1, 2):
            if j < RELAYED and dx == (-1 if j % 2 == 0 else 1):
                continue
            block = at_tenant(Z_ORDER[j], dx)
            wait_block(block)
    loads[2].wait()
    loads[3].wait()

    pick = (
        slot_key[...] == t * SLOTS + lax.broadcasted_iota(I32, (SLOTS, rows), 0)
    ).astype(BF16)
    picked = jnp.dot(pick, g[...], preferred_element_type=F32).astype(BF16)
    part = jnp.transpose(jnp.dot(picked, vq[...], preferred_element_type=F32)).astype(BF16)
    for i in range(n_tensor):
        rank_out[i % NC, i // NC * rank_local:(i // NC + 1) * rank_local, :] = (
            part[i * rank_local:(i + 1) * rank_local, :]
        )
    to_sibling = remote(rank_out.at[1 - c], rank_sib, q_send, q_recv, (t, sibling))
    to_sibling.start()
    to_sibling.wait()
    rank_sum[...] = (rank_out[c].astype(F32) + rank_sib[...].astype(F32)).astype(BF16)

    for dy in Y_FAR_FIRST:
        to = (y + dy + ny) % ny
        remote(
            rank_sum.at[ranks_at(to)], rank_in.at[ranks_at(y)], r_send, r_recv, (t, at_tensor(dy))
        ).start()
    rank_in[ranks_at(y), :] = rank_sum[ranks_at(y), :]

    for dz in SPREAD_FIRST:
        hand_on(dz)
    for dz, dx in T_MIXED[:STRAIGHT_EARLY]:
        send_columns(dz, dx)
    step = NC * rows_s

    def shared(i, carry):
        here = pl.ds(pl.multiple_of(i * 2 * step, 2 * step), 2 * step)
        acc[here, :] = jnp.dot(g[here, :], w[...], preferred_element_type=F32)
        return carry

    lax.fori_loop(0, ny // 2, shared, 0)

    for dz in SPREAD_EARLY:
        hand_on(dz)
    wait_bytes(rank_in.at[pl.ds(0, (ny - 1) * rank_local)], r_recv)
    total = jnp.zeros((rank_local, SLOTS), F32)
    for i in range(ny):
        total = total + rank_in[i * rank_local:(i + 1) * rank_local, :].astype(F32)
    code[...] = total.astype(BF16)
    for dz, dx in T_FAR_FIRST:
        remote(code, codes.at[ranks_at(t)], c_send, c_recv, (at_tenant(dz, dx), s)).start()
    codes[ranks_at(t), :] = code[...]
    for dz in SPREAD_LATE:
        hand_on(dz)
    for dz, dx in T_MIXED[STRAIGHT_EARLY:]:
        send_columns(dz, dx)
    second.ur[ranks_at(t), :] = second.uq[t]

    others = pl.ds(0, (n_tenant - 1) * rank_local)
    wait_bytes(codes.at[others], c_recv)

    owner_lane = lax.broadcasted_iota(I32, (step, n_tenant * rank_local), 1) // rank_local

    def mix(dy):
        d = (y + dy + ny) % ny
        here = pl.ds(pl.multiple_of(d * step, step), step)
        spread_codes = lax.dot_general(
            slot_hot[here, :], codes[...], (((1,), (1,)), ((), ())), preferred_element_type=F32
        )
        owner = row_owner[here, :]
        owner = jnp.concatenate([owner] * (n_tenant * rank_local // 128), axis=1)
        mixed[here, :] = jnp.where(owner == owner_lane, spread_codes, 0.0).astype(BF16)

    for dy in MIXED_FIRST:
        mix(dy)
    wait_bytes(first.ur.at[pl.ds(0, nz * (NX - 1) * rank_local)], first.u_recv)

    pieces = rows_s // PIECE
    low, high = range(pieces // 2), range(pieces // 2, pieces)

    def reduce_part(part, start, width):
        span = slice(start, start + width)

        def terms(dy):
            d = (y + dy + ny) % ny
            here = pl.ds(pl.multiple_of(d * step, step), step)
            if part is first and dy not in MIXED_FIRST:
                mix(dy)
            acc[here, span] = acc[here, span] + jnp.dot(
                mixed[here, :], part.ur[...], preferred_element_type=F32
            )
            theirs = pl.ds(pl.multiple_of(d * step + (1 - c) * rows_s, rows_s), rows_s)
            part.sib_out[d] = acc[theirs, span].astype(BF16)
            remote(
                part.sib_out.at[d], part.sib_in.at[d], part.x_send, part.x_recv.at[d], (t, sibling)
            ).start()

        def sibling_ready(dy):
            d = (y + dy + ny) % ny
            wait_bytes(part.sib_in.at[d], part.x_recv.at[d])

        def chip_sum(dy, p):
            d = (y + dy + ny) % ny
            here = pl.ds(pl.multiple_of(d * step + c * rows_s + p * PIECE, PIECE), PIECE)
            return acc[here, span] + part.sib_in[d, p * PIECE:(p + 1) * PIECE, :].astype(F32)

        def lines(h, p):
            return pl.ds(h * rows_s + p * PIECE, PIECE)

        def ring(way):
            return (part.ring_up, part.up_send, part.up_recv, (t, y_up)) if way > 0 else (
                part.ring_dn, part.dn_send, part.dn_recv, (t, y_dn)
            )

        def push(way, source, h, p):
            slots, send, recv, to = ring(way)
            remote(source, slots.at[lines(h, p)], send, recv.at[h, p], to).start()

        def fresh(way, p):
            slots = ring(way)[0]
            slots[lines(0, p), :] = chip_sum(3 * way, p).astype(BF16)
            push(way, slots.at[lines(0, p)], 1, p)

        def arrived(way, h, p):
            slots, send, recv, to = ring(way)
            wait_bytes(slots.at[lines(h, p)], recv.at[h, p])
            return slots[lines(h, p), :].astype(F32)

        def forward(way, h, p):
            slots = ring(way)[0]
            slots[lines(h, p), :] = (arrived(way, h, p) + chip_sum((3 - h) * way, p)).astype(BF16)
            push(way, slots.at[lines(h, p)], h + 1, p)

        terms(4)
        terms(3)
        sibling_ready(4)
        for p in range(pieces):
            part.stage[p * PIECE:(p + 1) * PIECE, :] = chip_sum(4, p).astype(BF16)
            push(1 if p in low else -1, part.stage.at[pl.ds(p * PIECE, PIECE)], 0, p)
        terms(-3)
        sibling_ready(3)
        for p in high:
            fresh(1, p)
        terms(2)
        sibling_ready(-3)
        for p in low:
            fresh(-1, p)
        terms(-2)
        terms(1)
        yield
        for p in range(pieces // 2):
            forward(1, 0, low[p])
            forward(-1, 0, high[p])
        terms(-1)
        sibling_ready(2)
        sibling_ready(-2)
        yield
        for p in range(pieces):
            forward(1, 1, (p + pieces // 2) % pieces)
            forward(-1, 1, p)
        terms(0)
        sibling_ready(1)
        sibling_ready(-1)
        yield
        for p in range(pieces):
            forward(1, 2, (p + pieces // 2) % pieces)
            forward(-1, 2, p)
        sibling_ready(0)
        yield
        for i in range(pieces):
            p = (i // 2 + (i % 2) * (pieces // 2)) % pieces
            out[p * PIECE:(p + 1) * PIECE, span] = (
                arrived(1, 3, p) + arrived(-1, 3, p) + chip_sum(0, p)
            ).astype(BF16)
        yield

    sums = [reduce_part(*each) for each in zip(parts, starts, widths)]
    for which in PART_ORDER:
        if which == 2:
            wait_bytes(second.ur.at[others], second.u_recv)
            continue
        next(sums[which])

    wait_bytes(g.at[pl.ds(0, (n_tenant - 1) * rows_t)], a_send)
    wait_bytes(uz.at[pl.ds(0, nz - 1)], uz_send)
    wait_bytes(first.ur.at[pl.ds(0, nz * (NX - 1) * rank_local)], first.u_send)
    wait_bytes(second.ur.at[others], second.u_send)
    wait_bytes(rank_in.at[pl.ds(0, (ny - 1) * rank_local)], r_send)
    wait_bytes(codes.at[others], c_send)
    for part in parts:
        wait_bytes(part.sib_out, part.x_send)
        wait_bytes(part.ring_up.at[pl.ds(0, 3 * rows_s + rows_s // 2)], part.up_send)
        wait_bytes(part.ring_dn.at[pl.ds(0, 3 * rows_s + rows_s // 2)], part.dn_send)


def on_device(
    n_tenant, n_tensor,
    activations, base_weight, v_codes, u_codes, group_bits, v_scale, u_scale, tenant_of, owner_map,
):
    rows_t, depth = activations.shape
    cols = base_weight.shape[1]
    rows = tenant_of.shape[0]
    full_rank = v_codes.shape[2]
    rank_local = u_codes.shape[1]
    rows_s = rows // n_tensor
    ny = n_tensor // NC
    all_ranks = n_tenant * rank_local
    vmem = pl.BlockSpec(memory_space=pltpu.VMEM)
    smem = pl.BlockSpec(memory_space=pltpu.SMEM)
    hbm = pl.BlockSpec(memory_space=pl.ANY)
    dma = pltpu.SemaphoreType.DMA
    pieces = rows_s // PIECE
    widths = (cols // 256 * 128 + 128, cols - cols // 256 * 128 - 128)
    return pl.pallas_call(
        functools.partial(kernel, n_tenant=n_tenant, n_tensor=n_tensor, widths=widths),
        out_shape=jax.ShapeDtypeStruct((rows_s, cols), BF16),
        in_specs=[hbm, hbm, hbm, hbm, smem, vmem, vmem, vmem, smem],
        out_specs=vmem,
        scratch_shapes=[
            pltpu.VMEM((rows, depth), BF16),
            pltpu.VMEM((depth, cols), BF16),
            pltpu.VMEM((depth, full_rank), I32),
            pltpu.VMEM(u_codes.shape[1:], I32),
            pltpu.VMEM((depth, full_rank), BF16),
            pltpu.VMEM((NC, full_rank // NC, SLOTS), BF16),
            pltpu.VMEM((full_rank // NC, SLOTS), BF16),
            pltpu.VMEM((full_rank // NC, SLOTS), BF16),
            pltpu.VMEM((full_rank // NC, SLOTS), BF16),
            pltpu.VMEM((rank_local, SLOTS), BF16),
            pltpu.VMEM((all_ranks, SLOTS), BF16),
            pltpu.VMEM((rows, SLOTS), BF16),
            pltpu.VMEM((rows, 128), I32),
            pltpu.VMEM((1, rows), I32),
            pltpu.VMEM((rows, all_ranks), BF16),
            pltpu.VMEM((rows, cols), F32),
            pltpu.VMEM((n_tenant // NX, NX, rank_local, widths[0]), BF16),
            dma((4,)), dma, dma((n_tenant,)), dma, dma((n_tenant // NX,)), dma, dma, dma, dma,
            dma, dma, pltpu.SemaphoreType.REGULAR((3,)),
            *[pltpu.VMEM((n_tenant, rank_local, width), BF16) for width in widths],
            *[pltpu.VMEM((all_ranks, width), BF16) for width in widths],
            *[pltpu.VMEM((ny, rows_s, width), BF16) for width in widths],
            *[pltpu.VMEM((ny, rows_s, width), BF16) for width in widths],
            *[pltpu.VMEM((rows_s, width), BF16) for width in widths],
            *[pltpu.VMEM((4 * rows_s, width), BF16) for width in widths],
            *[pltpu.VMEM((4 * rows_s, width), BF16) for width in widths],
            dma, dma, dma, dma, dma, dma, dma((ny,)), dma((ny,)),
            dma, dma, dma((4, pieces)), dma((4, pieces)),
            dma, dma, dma((4, pieces)), dma((4, pieces)),
        ],
        compiler_params=pltpu.CompilerParams(
            collective_id=0, has_side_effects=True, vmem_limit_bytes=58 * 1024 * 1024
        ),
        name="up_projection",
    )(
        activations, base_weight, v_codes, u_codes, group_bits, v_scale, u_scale,
        tenant_of.reshape(1, rows), owner_map,
    )


def solution(mesh):
    in_specs = (
        P("tenant", "tensor"),
        P("tensor", "tenant"),
        P("tenant", "tensor", None),
        P("tenant", "tensor", None),
        P("tenant", None),
        P("tenant", None),
        P("tenant", "tensor"),
        P(),
        P(),
    )
    return jax.shard_map(
        functools.partial(on_device, mesh.shape["tenant"], mesh.shape["tensor"]),
        mesh=mesh, in_specs=in_specs, out_specs=P("tensor", "tenant"), check_vma=False,
    )
```
